512 devices in a mesh: layer: 8 (over y, x_hi), latent: 64 (over z, x_lo, core).
Axes of the slice: x: 4 (x_hi: 2, x_lo: 2; x = x_hi * 2 + x_lo), y: 4, z: 16, core: 2. Of those that a mesh axis runs over, the one named last changes fastest.
Arguments:
- acts: bfloat16 [1280, 4608], P(None, 'layer'), may hold values from -6 to 6
- enc_weight: bfloat16 [4608, 32768], P('layer', 'latent'), may hold values from -0.09375 to 0.09375
- enc_bias: float32 [32768], P('latent'), may hold values from -3 to 3
- dec_weight: bfloat16 [32768, 4608], P('latent', 'layer'), may hold values from -0.3314563 to 0.3314563, as said below
- dec_bias: float32 [4608], P('layer'), may hold values from -2 to 2
Outputs:
- grad_enc: float32 [4608, 32768], P('layer', 'latent')
- grad_enc_bias: float32 [32768], P('latent')
- grad_dec: float32 [32768, 4608], P('latent', 'layer')
- grad_dec_bias: float32 [4608], P('layer')
The draws below stay inside these ranges and needn't reach their ends.
Inputs may be any that keep to these rules, and one draw needn't show every extreme that they name: `dec_weight`: decoder entries lie within 60 / sqrt(32768) of zero.
All inputs are finite; a program needn't handle non-finite values.
Results may differ from the reference program's by a relative error of at most 0.0045.
Values may be sent and summed in bfloat16 or wider, within the bound.
No kernel may reach another device: no remote copies, remote signals or barrier semaphores. Data moves between devices by JAX's collectives and lax.ppermute only.
A program may use at most 64 MiB of HBM per device.

```python
import math
import jax
import jax.numpy as jnp
from jax import lax

D = 2304
LAYERS = 2
LATENTS = 32768
ROWS = 1280
FEAT = 4608


def draw_dec_weight(key, part):
    key = jax.random.fold_in(key, 11)
    key_rows, key_base = jax.random.split(key, 2)
    width = LAYERS * D
    row_scale = jnp.exp(jax.random.uniform(key_rows, (LATENTS, 1), jnp.float32) * math.log(10.0))
    position = jnp.arange(width).astype(jnp.float32) / (width - 1)
    col_scale = jnp.exp(position * math.log(3.0))[None, :]
    base = jnp.clip(jax.random.normal(key_base, (LATENTS, width), jnp.float32), -6.0, 6.0)
    values = base * row_scale * col_scale / (3.0 * math.sqrt(LATENTS))
    return values.astype(jnp.bfloat16)


def levels(stream_key, shape, cuts, least, largest):
    loudness = 1.0
    for dim, parts in cuts:
        steps = jax.random.uniform(jax.random.fold_in(jax.random.fold_in(stream_key, 6), dim), (parts,), jnp.float32, least / len(cuts), largest / len(cuts))
        loudness = loudness * jnp.repeat(jnp.exp(steps), shape[dim] // parts).reshape((-1,) + (1,) * (len(shape) - 1 - dim))
    return loudness


def bell_draw(rng, extent, scale, limit, cuts=(), dtype=jnp.bfloat16):
    values = jax.random.normal(rng, extent, jnp.float32) * scale
    if len(cuts) > 0:
        values = levels(rng, extent, cuts, -0.22, 0.18) * values
    return jnp.clip(values, min=-limit, max=limit).astype(dtype)


def setup_inputs(seed: int = 0) -> dict:
    arg_keys = jax.random.split(jax.random.key(seed), 6)
    return {
        "acts": bell_draw(arg_keys[0], (ROWS, FEAT), 1.0, 6.0, ((1, 8),)),
        "enc_weight": bell_draw(arg_keys[1], (FEAT, LATENTS), FEAT ** -0.5, 0.09375, ((0, 8), (1, 64))),
        "enc_bias": bell_draw(arg_keys[2], (LATENTS,), 0.5, 3.0, ((0, 64),), jnp.float32),
        "dec_weight": draw_dec_weight(jax.random.fold_in(arg_keys[5], 71), 0),
        "dec_bias": bell_draw(arg_keys[4], (FEAT,), 0.3, 2.0, ((0, 8),), jnp.float32),
    }


def reference(acts, enc_weight, enc_bias, dec_weight, dec_bias):
    scale = 1.0 / jnp.sqrt(jnp.float32(ROWS))
    sparsity = 1.0
    pre = jnp.dot(acts, enc_weight, preferred_element_type=jnp.float32) + enc_bias
    codes = jax.nn.softplus(pre).astype(jnp.bfloat16)
    slope = jax.nn.sigmoid(pre)
    dec_f = dec_weight.astype(jnp.float32)
    norms = jnp.sqrt(lax.optimization_barrier(jnp.sum(dec_f * dec_f, axis=1)) + 1e-06)
    recon = jnp.dot(codes, dec_weight, preferred_element_type=jnp.float32) + dec_bias
    err_grad = (2.0 * scale * (recon - acts.astype(jnp.float32))).astype(jnp.bfloat16)
    grad_dec_bias = lax.optimization_barrier(jnp.sum(err_grad.astype(jnp.float32), axis=0))
    column = lax.optimization_barrier(jnp.sum(codes.astype(jnp.float32), axis=0))
    grad_dec = lax.dot_general(codes, err_grad, (((0,), (0,)), ((), ())), preferred_element_type=jnp.float32)
    grad_dec = grad_dec + (sparsity * scale * column / norms)[:, None] * dec_f
    back = lax.dot_general(err_grad, dec_weight, (((1,), (1,)), ((), ())), preferred_element_type=jnp.float32)
    back = back + sparsity * scale * norms
    delta = (back * slope).astype(jnp.bfloat16)
    grad_enc = lax.dot_general(acts, delta, (((0,), (0,)), ((), ())), preferred_element_type=jnp.float32)
    grad_enc_bias = lax.optimization_barrier(jnp.sum(delta.astype(jnp.float32), axis=0))
    return (grad_enc, grad_enc_bias, grad_dec, grad_dec_bias)
```

```python
import jax
import jax.numpy as jnp
from jax import lax
from jax.sharding import PartitionSpec as P

NZ, NXL, NC = 16, 2, 2
ZLO = 4
ZHI = NZ // ZLO


def latent_index(z, xl, c):
    return (z * NXL + xl) * NC + c


NEAR = [
    [latent_index(zh * ZLO + zl, xl, c) for zl in range(ZLO) for xl in range(NXL)]
    for zh in range(ZHI)
    for c in range(NC)
]
FAR = [
    [latent_index(zh * ZLO + zl, xl, c) for zh in range(ZHI)]
    for zl in range(ZLO)
    for xl in range(NXL)
    for c in range(NC)
]
CORE = [
    (latent_index(z, xl, c), latent_index(z, xl, 1 - c))
    for z in range(NZ)
    for xl in range(NXL)
    for c in range(NC)
]

F32 = jnp.float32
BF16 = jnp.bfloat16


def dot(a, b, dims):
    return lax.dot_general(a, b, (dims, ((), ())), preferred_element_type=F32)


def add_up(blocks, me, own):
    total = own
    for j in range(blocks.shape[0]):
        total = total + jnp.where(me == j, 0.0, blocks[j].astype(F32))
    return total


def per_device(acts, enc_weight, enc_bias, dec_weight, dec_bias):
    rows, feat = acts.shape
    lat = enc_weight.shape[1]
    scale = 1.0 / jnp.sqrt(F32(rows))
    sparsity = 1.0
    me_layer = lax.axis_index("layer")
    me_latent = lax.axis_index("latent")
    n_layer = 8
    part = rows // n_layer
    core = me_latent % NC
    near = (me_latent // NC) % (ZLO * NXL)
    half = rows // NC
    block = half // (ZLO * NXL)

    with jax.named_scope("norms"):
        dec_f = dec_weight.astype(F32)
        squares = jnp.sum(dec_f * dec_f, axis=1)
        norms = jnp.sqrt(lax.psum(squares, "layer") + 1e-06)

    with jax.named_scope("encode"):
        partial_pre = dot(acts, enc_weight, ((1,), (0,))).astype(BF16)
        got = lax.all_to_all(partial_pre, "layer", 0, 0, tiled=True)
        own_acts = lax.dynamic_slice_in_dim(acts, me_layer * part, part, 0)
        own_pre = dot(own_acts, enc_weight, ((1,), (0,)))
        pre = add_up(got.reshape(n_layer, part, lat), me_layer, own_pre) + enc_bias
        codes_part = jax.nn.softplus(pre).astype(BF16)
        slope = jax.nn.sigmoid(pre)
        codes = lax.all_to_all(
            jnp.broadcast_to(codes_part, (n_layer, part, lat)).reshape(rows, lat),
            "layer", 0, 0, tiled=True,
        )

    with jax.named_scope("decode"):
        other_codes = lax.dynamic_slice_in_dim(codes, (1 - core) * half, half, 0)
        core_codes = lax.dynamic_slice_in_dim(codes, core * half, half, 0)
        away = dot(other_codes, dec_weight, ((1,), (0,))).astype(BF16)
        arrived = lax.ppermute(away, "latent", CORE)
        recon = dot(core_codes, dec_weight, ((1,), (0,))) + arrived.astype(F32)
        got = lax.all_to_all(
            recon.astype(BF16), "latent", 0, 0, axis_index_groups=NEAR, tiled=True
        )
        own_recon = lax.dynamic_slice_in_dim(recon, near * block, block, 0)
        recon = add_up(got.reshape(ZLO * NXL, block, feat), near, own_recon).astype(BF16)
        got = lax.all_to_all(
            jnp.broadcast_to(recon, (ZHI, block, feat)).reshape(ZHI * block, feat),
            "latent", 0, 0, axis_index_groups=FAR, tiled=True,
        )
        recon = jnp.sum(got.reshape(ZHI, block, feat).astype(F32), axis=0) + dec_bias
        acts_part = lax.dynamic_slice_in_dim(acts, core * half + near * block, block, 0)
        err_part = (2.0 * scale * (recon - acts_part.astype(F32))).astype(BF16)

    with jax.named_scope("spread_error"):
        err_half = lax.all_to_all(
            jnp.broadcast_to(err_part, (ZLO * NXL, block, feat)).reshape(half, feat),
            "latent", 0, 0, axis_index_groups=NEAR, tiled=True,
        )
        err_other = lax.ppermute(err_half, "latent", CORE)
        first = jnp.where(core == 0, err_half, err_other)
        second = jnp.where(core == 0, err_other, err_half)
        err_grad = jnp.concatenate([first, second], axis=0)

    with jax.named_scope("back"):
        partial_back = dot(err_grad, dec_weight, ((1,), (1,))).astype(BF16)
        got = lax.all_to_all(partial_back, "layer", 0, 0, tiled=True)
        own_err = lax.dynamic_slice_in_dim(err_grad, me_layer * part, part, 0)
        own_back = dot(own_err, dec_weight, ((1,), (1,)))
        back = add_up(got.reshape(n_layer, part, lat), me_layer, own_back)
        back = back + sparsity * scale * norms
        delta_part = (back * slope).astype(BF16)
        delta = lax.all_to_all(
            jnp.broadcast_to(delta_part, (n_layer, part, lat)).reshape(rows, lat),
            "layer", 0, 0, tiled=True,
        )

    with jax.named_scope("grads"):
        grad_dec_bias = jnp.sum(err_grad.astype(F32), axis=0)
        column = jnp.sum(codes.astype(F32), axis=0)
        grad_dec = dot(codes, err_grad, ((0,), (0,)))
        grad_dec = grad_dec + (sparsity * scale * column / norms)[:, None] * dec_f
        grad_enc = dot(acts, delta, ((0,), (0,)))
        grad_enc_bias = jnp.sum(delta.astype(F32), axis=0)
    return (grad_enc, grad_enc_bias, grad_dec, grad_dec_bias)


def solution(mesh):
    return jax.shard_map(
        per_device,
        mesh=mesh,
        in_specs=(
            P(None, "layer"),
            P("layer", "latent"),
            P("latent"),
            P("latent", "layer"),
            P("layer"),
        ),
        out_specs=(P("layer", "latent"), P("latent"), P("latent", "layer"), P("layer")),
        check_vma=False,
    )
```

```python
import jax
import jax.numpy as jnp
from jax import lax
from jax.sharding import PartitionSpec as P

NZ, NXL, NC = 16, 2, 2
NY, NXH = 4, 2
ZLO = 4
ZHI = NZ // ZLO


def latent_index(z, xl, c):
    return (z * NXL + xl) * NC + c


def layer_index(y, xh):
    return y * NXH + xh


NEAR = [
    [latent_index(zh * ZLO + zl, xl, c) for zl in range(ZLO) for xl in range(NXL)]
    for zh in range(ZHI)
    for c in range(NC)
]
FAR = [
    [latent_index(zh * ZLO + zl, xl, c) for zh in range(ZHI)]
    for zl in range(ZLO)
    for xl in range(NXL)
    for c in range(NC)
]
CORE = [
    (latent_index(z, xl, c), latent_index(z, xl, 1 - c))
    for z in range(NZ)
    for xl in range(NXL)
    for c in range(NC)
]
LAYER_STEPS = [
    [(layer_index(y, xh), layer_index(y ^ 1, xh)) for y in range(NY) for xh in range(NXH)],
    [(layer_index(y, xh), layer_index(3 - y, xh)) for y in range(NY) for xh in range(NXH)],
    [(layer_index(y, xh), layer_index(y, 1 - xh)) for y in range(NY) for xh in range(NXH)],
]

F32 = jnp.float32
BF16 = jnp.bfloat16


def dot(a, b, dims):
    return lax.dot_general(a, b, (dims, ((), ())), preferred_element_type=F32)


def add_up(blocks, me, own):
    total = own
    for j in range(blocks.shape[0]):
        total = total + jnp.where(me == j, 0.0, blocks[j].astype(F32))
    return total


def per_device(acts, enc_weight, enc_bias, dec_weight, dec_bias):
    rows, feat = acts.shape
    lat = enc_weight.shape[1]
    scale = 1.0 / jnp.sqrt(F32(rows))
    sparsity = 1.0
    me_layer = lax.axis_index("layer")
    me_latent = lax.axis_index("latent")
    n_layer = NY * NXH
    n_near = ZLO * NXL
    part = rows // n_layer
    core = me_latent % NC
    near = (me_latent // NC) % n_near
    half = rows // NC
    block = feat // n_near

    with jax.named_scope("local_rows"):
        acts = jnp.concatenate(
            [
                lax.dynamic_slice_in_dim(acts, core * half, half, 0),
                lax.dynamic_slice_in_dim(acts, (1 - core) * half, half, 0),
            ],
            axis=0,
        )

    with jax.named_scope("encode"):
        partial_pre = dot(acts, enc_weight, ((1,), (0,))).astype(BF16)
        got = lax.all_to_all(partial_pre, "layer", 0, 0, tiled=True)
        own_acts = lax.dynamic_slice_in_dim(acts, me_layer * part, part, 0)
        own_pre = dot(own_acts, enc_weight, ((1,), (0,)))
        pre = add_up(got.reshape(n_layer, part, lat), me_layer, own_pre) + enc_bias
        codes_part = jax.nn.softplus(pre).astype(BF16)
        slope = jax.nn.sigmoid(pre)
        codes = lax.all_to_all(
            jnp.broadcast_to(codes_part, (n_layer, part, lat)).reshape(rows, lat),
            "layer", 0, 0, tiled=True,
        )

    with jax.named_scope("norms"):
        dec_f = dec_weight.astype(F32)
        squares = jnp.sum(dec_f * dec_f, axis=1)
        squares, _ = lax.optimization_barrier((squares, codes_part))
        for pairs in LAYER_STEPS:
            squares = squares + lax.ppermute(squares, "layer", pairs)
        norms = jnp.sqrt(squares + 1e-06)

    with jax.named_scope("decode"):
        away = dot(dec_weight, codes[half:], ((0,), (1,))).astype(BF16)
        arrived = lax.ppermute(away, "latent", CORE)
        recon = lax.optimization_barrier(dot(dec_weight, codes[:half], ((0,), (1,))))
        recon = recon + arrived.astype(F32)
        got = lax.all_to_all(
            recon.astype(BF16), "latent", 0, 0, axis_index_groups=NEAR, tiled=True
        )
        own_recon = lax.dynamic_slice_in_dim(recon, near * block, block, 0)
        recon = add_up(got.reshape(n_near, block, half), near, own_recon).astype(BF16)
        got = lax.all_to_all(
            jnp.broadcast_to(recon, (ZHI, block, half)).reshape(ZHI * block, half),
            "latent", 0, 0, axis_index_groups=FAR, tiled=True,
        )
        own_bias = lax.dynamic_slice_in_dim(dec_bias, near * block, block, 0)
        recon = jnp.sum(got.reshape(ZHI, block, half).astype(F32), axis=0) + own_bias[:, None]
        acts_part = lax.dynamic_slice(acts, (0, near * block), (half, block)).T
        err_part = (2.0 * scale * (recon - acts_part.astype(F32))).astype(BF16)

    with jax.named_scope("spread_error"):
        err_own = lax.all_to_all(
            jnp.broadcast_to(err_part, (n_near, block, half)).reshape(feat, half),
            "latent", 0, 0, axis_index_groups=NEAR, tiled=True,
        )
        err_other = lax.ppermute(err_own, "latent", CORE)
        err_grad = jnp.concatenate([err_own, err_other], axis=1)

    with jax.named_scope("back"):
        partial_back = dot(err_grad, dec_weight, ((0,), (1,))).astype(BF16)
        got = lax.all_to_all(partial_back, "layer", 0, 0, tiled=True)
        own_err = lax.dynamic_slice_in_dim(err_grad, me_layer * part, part, 1)
        own_back = dot(own_err, dec_weight, ((0,), (1,)))
        back = add_up(got.reshape(n_layer, part, lat), me_layer, own_back)
        back = back + sparsity * scale * norms
        delta_part = (back * slope).astype(BF16)
        delta = lax.all_to_all(
            jnp.broadcast_to(delta_part, (n_layer, part, lat)).reshape(rows, lat),
            "layer", 0, 0, tiled=True,
        )

    with jax.named_scope("grads"):
        grad_dec_bias = jnp.sum(err_own.astype(F32), axis=1) + jnp.sum(err_other.astype(F32), axis=1)
        column = jnp.sum(codes.astype(F32), axis=0)
        grad_dec = dot(codes, err_grad, ((0,), (1,)))
        grad_dec = grad_dec + (sparsity * scale * column / norms)[:, None] * dec_f
        grad_enc = dot(acts, delta, ((0,), (0,)))
        grad_enc_bias = jnp.sum(delta.astype(F32), axis=0)
    return (grad_enc, grad_enc_bias, grad_dec, grad_dec_bias)


def solution(mesh):
    return jax.shard_map(
        per_device,
        mesh=mesh,
        in_specs=(
            P(None, "layer"),
            P("layer", "latent"),
            P("latent"),
            P("latent", "layer"),
            P("layer"),
        ),
        out_specs=(P("layer", "latent"), P("latent"), P("latent", "layer"), P("layer")),
        check_vma=False,
    )
```

```python
import jax
import jax.numpy as jnp
from jax import lax
from jax.sharding import PartitionSpec as P

NZ, NXL, NC = 16, 2, 2
NY, NXH = 4, 2
ZLO = 4
ZHI = NZ // ZLO


def latent_index(z, xl, c):
    return (z * NXL + xl) * NC + c


def layer_index(y, xh):
    return y * NXH + xh


NEAR = [
    [latent_index((zh * ZLO + zl - 2 * c) % NZ, xl, c) for zl in range(ZLO) for xl in range(NXL)]
    for zh in range(ZHI)
    for c in range(NC)
]
FAR = [
    [latent_index(zh * ZLO + zl, xl, c) for zh in range(ZHI)]
    for zl in range(ZLO)
    for xl in range(NXL)
    for c in range(NC)
]
CORE = [
    (latent_index(z, xl, c), latent_index(z, xl, 1 - c))
    for z in range(NZ)
    for xl in range(NXL)
    for c in range(NC)
]
LAYER_STEPS = [
    [(layer_index(y, xh), layer_index(y ^ 1, xh)) for y in range(NY) for xh in range(NXH)],
    [(layer_index(y, xh), layer_index(3 - y, xh)) for y in range(NY) for xh in range(NXH)],
    [(layer_index(y, xh), layer_index(y, 1 - xh)) for y in range(NY) for xh in range(NXH)],
]

F32 = jnp.float32
BF16 = jnp.bfloat16


def dot(a, b, dims):
    return lax.dot_general(a, b, (dims, ((), ())), preferred_element_type=F32)


def add_up(blocks, me, own):
    total = own
    for j in range(blocks.shape[0]):
        total = total + jnp.where(me == j, 0.0, blocks[j].astype(F32))
    return total


def spread(x, n):
    return jnp.broadcast_to(x, (n,) + x.shape).reshape((n * x.shape[0],) + x.shape[1:])


def per_device(acts, enc_weight, enc_bias, dec_weight, dec_bias):
    rows, feat = acts.shape
    lat = enc_weight.shape[1]
    scale = 1.0 / jnp.sqrt(F32(rows))
    sparsity = 1.0
    me_layer = lax.axis_index("layer")
    me_latent = lax.axis_index("latent")
    n_layer = NY * NXH
    n_near = ZLO * NXL
    part = lat // n_layer
    core = lax.rem(me_latent, NC)
    x_lo = lax.rem(lax.div(me_latent, NC), NXL)
    z = lax.div(me_latent, NC * NXL)
    near = lax.rem(z + 2 * core, ZLO) * NXL + x_lo
    half = rows // NC
    block = feat // n_near

    with jax.named_scope("local_rows"):
        acts_t = acts.T
        acts_t = jnp.concatenate(
            [
                lax.dynamic_slice_in_dim(acts_t, core * half, half, 1),
                lax.dynamic_slice_in_dim(acts_t, (1 - core) * half, half, 1),
            ],
            axis=1,
        )
        dec_t = dec_weight.T

    with jax.named_scope("encode"):
        partial_pre = dot(enc_weight, acts_t, ((0,), (0,))).astype(BF16)
        got = lax.all_to_all(partial_pre, "layer", 0, 0, tiled=True)
        own_enc = lax.dynamic_slice_in_dim(enc_weight, me_layer * part, part, 1)
        own_pre = lax.optimization_barrier(dot(own_enc, acts_t, ((0,), (0,))))
        own_bias = lax.dynamic_slice_in_dim(enc_bias, me_layer * part, part, 0)
        pre = add_up(got.reshape(n_layer, part, rows), me_layer, own_pre) + own_bias[:, None]
        codes_part = jax.nn.softplus(pre).astype(BF16)
        slope = jax.nn.sigmoid(pre)
        codes = lax.all_to_all(spread(codes_part, n_layer), "layer", 0, 0, tiled=True)

    with jax.named_scope("decode"):
        away = dot(dec_t, codes[:, half:], ((1,), (0,))).astype(BF16)
        arrived = lax.ppermute(away, "latent", CORE)
        recon = lax.optimization_barrier(dot(dec_t, codes[:, :half], ((1,), (0,))))
        recon = recon + arrived.astype(F32)
        got = lax.all_to_all(
            recon.astype(BF16), "latent", 0, 0, axis_index_groups=NEAR, tiled=True
        )
        own_recon = lax.dynamic_slice_in_dim(recon, near * block, block, 0)
        recon = add_up(got.reshape(n_near, block, half), near, own_recon).astype(BF16)

    with jax.named_scope("norms"):
        dec_f = dec_t.astype(F32)
        squares = jnp.sum(dec_f * dec_f, axis=0)
        squares, recon = lax.optimization_barrier((squares, recon))
        for pairs in LAYER_STEPS:
            squares = squares + lax.ppermute(squares, "layer", pairs)
        norms = jnp.sqrt(squares + 1e-06)

    with jax.named_scope("error"):
        got = lax.all_to_all(
            spread(recon, ZHI), "latent", 0, 0, axis_index_groups=FAR, tiled=True
        )
        own_dec_bias = lax.dynamic_slice_in_dim(dec_bias, near * block, block, 0)
        acts_part = lax.dynamic_slice(acts_t, (near * block, 0), (block, half))
        recon = jnp.sum(got.reshape(ZHI, block, half).astype(F32), axis=0) + own_dec_bias[:, None]
        err_part = (2.0 * scale * (recon - acts_part.astype(F32))).astype(BF16)
        err_part, norms = lax.optimization_barrier((err_part, norms))
        err_own = lax.all_to_all(
            spread(err_part, n_near), "latent", 0, 0, axis_index_groups=NEAR, tiled=True
        )
        err_other = lax.ppermute(err_own, "latent", CORE)
        err_t = jnp.concatenate([err_own, err_other], axis=1)

    with jax.named_scope("back"):
        partial_back = dot(dec_t, err_t, ((0,), (0,))).astype(BF16)
        got = lax.all_to_all(partial_back, "layer", 0, 0, tiled=True)
        own_dec = lax.dynamic_slice_in_dim(dec_t, me_layer * part, part, 1)
        own_back = lax.optimization_barrier(dot(own_dec, err_t, ((0,), (0,))))
        own_norms = lax.dynamic_slice_in_dim(norms, me_layer * part, part, 0)
        back = add_up(got.reshape(n_layer, part, rows), me_layer, own_back)
        back = back + (sparsity * scale * own_norms)[:, None]
        delta_part = (back * slope).astype(BF16)
        delta = lax.all_to_all(spread(delta_part, n_layer), "layer", 0, 0, tiled=True)

    with jax.named_scope("grads"):
        grad_dec_bias = jnp.sum(err_own.astype(F32), axis=1) + jnp.sum(err_other.astype(F32), axis=1)
        column = jnp.sum(codes.astype(F32), axis=1)
        grad_dec = dot(err_t, codes, ((1,), (1,)))
        grad_dec = grad_dec + (sparsity * scale * column / norms)[None, :] * dec_f
        grad_enc = dot(acts_t, delta, ((1,), (1,)))
        grad_enc_bias = jnp.sum(delta.astype(F32), axis=1)
    return (grad_enc, grad_enc_bias, grad_dec.T, grad_dec_bias)


def solution(mesh):
    return jax.shard_map(
        per_device,
        mesh=mesh,
        in_specs=(
            P(None, "layer"),
            P("layer", "latent"),
            P("latent"),
            P("latent", "layer"),
            P("layer"),
        ),
        out_specs=(P("layer", "latent"), P("latent"), P("latent", "layer"), P("layer")),
        check_vma=False,
    )
```

```python
import jax
import jax.numpy as jnp
from jax import lax
from jax.experimental import pallas as pl
from jax.experimental.pallas import tpu as pltpu
from jax.sharding import PartitionSpec as P

NZ, NXL, NC = 16, 2, 2
NY, NXH = 4, 2
ZLO = 4
ZHI = NZ // ZLO


def latent_index(z, xl, c):
    return (z * NXL + xl) * NC + c


def layer_index(y, xh):
    return y * NXH + xh


NEAR = [
    [latent_index((zh * ZLO + zl - 2 * c) % NZ, xl, c) for zl in range(ZLO) for xl in range(NXL)]
    for zh in range(ZHI)
    for c in range(NC)
]
FAR = [
    [latent_index(zh * ZLO + zl, xl, c) for zh in range(ZHI)]
    for zl in range(ZLO)
    for xl in range(NXL)
    for c in range(NC)
]
CORE = [
    (latent_index(z, xl, c), latent_index(z, xl, 1 - c))
    for z in range(NZ)
    for xl in range(NXL)
    for c in range(NC)
]
LAYER_STEPS = [
    [(layer_index(y, xh), layer_index(y ^ 1, xh)) for y in range(NY) for xh in range(NXH)],
    [(layer_index(y, xh), layer_index(3 - y, xh)) for y in range(NY) for xh in range(NXH)],
    [(layer_index(y, xh), layer_index(y, 1 - xh)) for y in range(NY) for xh in range(NXH)],
]

F32 = jnp.float32
BF16 = jnp.bfloat16


def dot(a, b, dims):
    return lax.dot_general(a, b, (dims, ((), ())), preferred_element_type=F32)


VMEM = pl.BlockSpec(memory_space=pltpu.VMEM)
SMEM = pl.BlockSpec(memory_space=pltpu.SMEM)


def local_call(body, name, **kwargs):
    params = pltpu.CompilerParams(vmem_limit_bytes=48 * 1024 * 1024)
    return pl.pallas_call(body, name=name, compiler_params=params, **kwargs)


def like(shape, dtype):
    return jax.ShapeDtypeStruct(shape, dtype)


def add_blocks(me, got, own):
    total = own
    for j in range(got.shape[0]):
        total = total + jnp.where(me == j, 0.0, got[j].astype(F32))
    return total


def encode(core, enc, acts_t):
    feat, lat = enc.shape
    rows = acts_t.shape[1]
    half = rows // NC

    def body(c, e, a, out):
        out[...] = dot(e[...], a[...], ((0,), (0,))).astype(BF16)

    return local_call(
        body, "encode",
        out_shape=like((lat, rows), BF16),
        grid_spec=pltpu.PrefetchScalarGridSpec(
            num_scalar_prefetch=1,
            grid=(NC,),
            in_specs=[
                pl.BlockSpec((feat, lat), lambda i, c: (0, 0)),
                pl.BlockSpec((feat, half), lambda i, c: (0, lax.rem(i + c[0], NC))),
            ],
            out_specs=pl.BlockSpec((lat, half), lambda i, c: (0, i)),
        ),
    )(core, enc, acts_t)


def activate(me, got, own, bias):
    n, part, rows = got.shape

    def body(m, g, o, b, codes, slope):
        pre = add_blocks(m[0], g, o[...]) + b[...]
        tail = jnp.exp(-jnp.abs(pre))
        value = (jnp.maximum(pre, 0.0) + jnp.log1p(tail)).astype(BF16)
        slope[...] = jnp.where(pre >= 0, 1.0, tail) / (1.0 + tail)
        for j in range(n):
            codes[j] = value

    return local_call(
        body, "activate",
        out_shape=(like((n, part, rows), BF16), like((part, rows), F32)),
        in_specs=[SMEM, VMEM, VMEM, VMEM],
        out_specs=(VMEM, VMEM),
    )(me, got, own, bias)


def merge_cores(near, own, arrived):
    n, block, half = own.shape

    def body(m, o, a, out, kept):
        for j in range(n):
            out[j] = (o[j] + a[j].astype(F32)).astype(BF16)
        kept[...] = o[m[0]] + a[m[0]].astype(F32)

    return local_call(
        body, "merge_cores",
        out_shape=(like((n, block, half), BF16), like((block, half), F32)),
        in_specs=[SMEM, VMEM, VMEM],
        out_specs=(VMEM, VMEM),
    )(near, own, arrived)


def near_sum(me, got, own, copies):
    block, half = own.shape

    def body(m, g, o, out):
        total = add_blocks(m[0], g, o[...]).astype(BF16)
        for j in range(copies):
            out[j] = total

    return local_call(
        body, "near_sum",
        out_shape=like((copies, block, half), BF16),
        in_specs=[SMEM, VMEM, VMEM],
        out_specs=VMEM,
    )(me, got, own)


def error(got, bias, acts, factor, copies):
    n, block, half = got.shape

    def body(f, g, b, a, out):
        recon = g[0].astype(F32)
        for j in range(1, n):
            recon = recon + g[j].astype(F32)
        err = (f[0] * (recon + b[...] - a[...].astype(F32))).astype(BF16)
        for j in range(copies):
            out[j] = err

    return local_call(
        body, "error",
        out_shape=like((copies, block, half), BF16),
        in_specs=[SMEM, VMEM, VMEM, VMEM],
        out_specs=VMEM,
    )(factor, got, bias, acts)


def back_half(dec_t, err, side, filled=None):
    feat, lat = dec_t.shape
    half = err.shape[1]

    def body(*refs):
        d, e, out = refs[0], refs[1], refs[-1]
        out[...] = dot(d[...], e[...], ((0,), (0,))).astype(BF16)

    args = [dec_t, err]
    specs = [
        pl.BlockSpec((feat, lat), lambda i: (0, 0)),
        pl.BlockSpec((feat, half), lambda i: (0, 0)),
    ]
    aliases = {}
    if filled is not None:
        args.append(filled)
        specs.append(pl.BlockSpec(memory_space=pl.ANY))
        aliases = {2: 0}
    return local_call(
        body, "back_half",
        out_shape=like((lat, NC * half), BF16),
        grid=(1,),
        in_specs=specs,
        out_specs=pl.BlockSpec((lat, half), lambda i: (0, side)),
        input_output_aliases=aliases,
    )(*args)


def weigh(me, got, own, penalty, slope):
    n, part, rows = got.shape

    def body(m, g, o, p, s, out):
        back = add_blocks(m[0], g, o[...]) + p[...]
        value = (back * s[...]).astype(BF16)
        for j in range(n):
            out[j] = value

    return local_call(
        body, "weigh",
        out_shape=like((n, part, rows), BF16),
        in_specs=[SMEM, VMEM, VMEM, VMEM, VMEM],
        out_specs=VMEM,
    )(me, got, own, penalty, slope)


def encoder_grads(acts_t, delta):
    feat, rows = acts_t.shape
    lat = delta.shape[0]

    def body(a, d, weight, bias):
        weight[...] = dot(a[...], d[...], ((1,), (1,)))
        bias[...] = dot(jnp.ones((8, rows), BF16), d[...], ((1,), (1,)))[:1]

    return local_call(
        body, "encoder_grads",
        out_shape=(like((feat, lat), F32), like((1, lat), F32)),
        in_specs=[VMEM, VMEM],
        out_specs=(VMEM, VMEM),
    )(acts_t, delta)


def exchange(x, axis, groups=None):
    return lax.all_to_all(x, axis, 0, 0, axis_index_groups=groups, tiled=True)


def per_device(acts, enc_weight, enc_bias, dec_weight, dec_bias):
    rows, feat = acts.shape
    lat = enc_weight.shape[1]
    scale = 1.0 / jnp.sqrt(F32(rows))
    sparsity = 1.0
    me_layer = lax.axis_index("layer")
    me_latent = lax.axis_index("latent")
    n_layer = NY * NXH
    n_near = ZLO * NXL
    part = lat // n_layer
    core = lax.rem(me_latent, NC)
    x_lo = lax.rem(lax.div(me_latent, NC), NXL)
    z = lax.div(me_latent, NC * NXL)
    near = lax.rem(z + 2 * core, ZLO) * NXL + x_lo
    half = rows // NC
    block = feat // n_near
    layer_ref = me_layer[None].astype(jnp.int32)
    near_ref = near[None].astype(jnp.int32)

    with jax.named_scope("encode"):
        partial_pre = encode(core[None].astype(jnp.int32), enc_weight, acts.T)
        got = exchange(partial_pre.reshape(n_layer, part, rows), "layer")
        acts_t = jnp.concatenate(
            [
                lax.dynamic_slice_in_dim(acts.T, core * half, half, 1),
                lax.dynamic_slice_in_dim(acts.T, (1 - core) * half, half, 1),
            ],
            axis=1,
        )
        own_enc = lax.dynamic_slice_in_dim(enc_weight, me_layer * part, part, 1)
        own_pre = dot(own_enc, acts_t, ((0,), (0,)))
        own_bias = lax.dynamic_slice_in_dim(enc_bias, me_layer * part, part, 0)
        codes_part, slope = activate(layer_ref, got, own_pre, own_bias[:, None])
        codes = exchange(codes_part, "layer").reshape(lat, rows)

    with jax.named_scope("decode"):
        dec_t = dec_weight.T
        away = dot(dec_t, codes[:, half:], ((1,), (0,))).astype(BF16)
        arrived = lax.ppermute(away, "latent", CORE)
        recon = dot(dec_t, codes[:, :half], ((1,), (0,)))
        shape = (n_near, block, half)
        recon, own_recon = merge_cores(near_ref, recon.reshape(shape), arrived.reshape(shape))
        got = exchange(recon, "latent", NEAR)
        recon = near_sum(near_ref, got, own_recon, ZHI)

    with jax.named_scope("norms"):
        dec_f = dec_t.astype(F32)
        squares = jnp.sum(dec_f * dec_f, axis=0)
        squares, recon = lax.optimization_barrier((squares, recon))
        for pairs in LAYER_STEPS:
            squares = squares + lax.ppermute(squares, "layer", pairs)
        norms = jnp.sqrt(squares + 1e-06)

    with jax.named_scope("error"):
        got = exchange(recon, "latent", FAR)
        own_dec_bias = lax.dynamic_slice_in_dim(dec_bias, near * block, block, 0)
        acts_part = lax.dynamic_slice(acts_t, (near * block, 0), (block, half))
        err = error(got, own_dec_bias[:, None], acts_part, (2.0 * scale)[None], n_near)
        err, norms = lax.optimization_barrier((err, norms))
        err_own = exchange(err, "latent", NEAR).reshape(feat, half)
        err_other = lax.ppermute(err_own, "latent", CORE)

    with jax.named_scope("back"):
        partial_back = back_half(dec_t, err_own, 0)
        partial_back = back_half(dec_t, err_other, 1, partial_back)
        got = exchange(partial_back.reshape(n_layer, part, rows), "layer")
        err_t = jnp.concatenate([err_own, err_other], axis=1)
        own_dec = lax.dynamic_slice_in_dim(dec_t, me_layer * part, part, 1)
        own_back = dot(own_dec, err_t, ((0,), (0,)))
        own_norms = lax.dynamic_slice_in_dim(norms, me_layer * part, part, 0)
        penalty = (sparsity * scale * own_norms)[:, None]
        delta_part = weigh(layer_ref, got, own_back, penalty, slope)
        delta = exchange(delta_part, "layer").reshape(lat, rows)

    with jax.named_scope("grads"):
        grad_dec_bias = jnp.sum(err_own.astype(F32), axis=1) + jnp.sum(err_other.astype(F32), axis=1)
        column = jnp.sum(codes.astype(F32), axis=1)
        grad_dec = dot(err_t, codes, ((1,), (1,)))
        grad_dec = grad_dec + (sparsity * scale * column / norms)[None, :] * dec_f
        grad_enc, grad_enc_bias = encoder_grads(acts_t, delta)
    return (grad_enc, grad_enc_bias.reshape(lat), grad_dec.T, grad_dec_bias)


def solution(mesh):
    return jax.shard_map(
        per_device,
        mesh=mesh,
        in_specs=(
            P(None, "layer"),
            P("layer", "latent"),
            P("latent"),
            P("latent", "layer"),
            P("layer"),
        ),
        out_specs=(P("layer", "latent"), P("latent"), P("latent", "layer"), P("layer")),
        check_vma=False,
    )
```

```python
import jax
import jax.numpy as jnp
from jax import lax
from jax.experimental import pallas as pl
from jax.experimental.pallas import tpu as pltpu
from jax.sharding import PartitionSpec as P

NZ, NXL, NC = 16, 2, 2
NY, NXH = 4, 2
ZLO = 4
ZHI = NZ // ZLO


def latent_index(z, xl, c):
    return (z * NXL + xl) * NC + c


def layer_index(y, xh):
    return y * NXH + xh


NEAR = [
    [latent_index((zh * ZLO + zl - 2 * c) % NZ, xl, c) for zl in range(ZLO) for xl in range(NXL)]
    for zh in range(ZHI)
    for c in range(NC)
]
FAR = [
    [latent_index(zh * ZLO + zl, xl, c) for zh in range(ZHI)]
    for zl in range(ZLO)
    for xl in range(NXL)
    for c in range(NC)
]
CORE = [
    (latent_index(z, xl, c), latent_index(z, xl, 1 - c))
    for z in range(NZ)
    for xl in range(NXL)
    for c in range(NC)
]
LAYER_STEPS = [
    [(layer_index(y, xh), layer_index(y ^ 1, xh)) for y in range(NY) for xh in range(NXH)],
    [(layer_index(y, xh), layer_index(3 - y, xh)) for y in range(NY) for xh in range(NXH)],
    [(layer_index(y, xh), layer_index(y, 1 - xh)) for y in range(NY) for xh in range(NXH)],
]

F32 = jnp.float32
BF16 = jnp.bfloat16


def dot(a, b, dims):
    return lax.dot_general(a, b, (dims, ((), ())), preferred_element_type=F32)


VMEM = pl.BlockSpec(memory_space=pltpu.VMEM)
SMEM = pl.BlockSpec(memory_space=pltpu.SMEM)
HBM = pl.BlockSpec(memory_space=pltpu.HBM)
ALONE = 58


def local_call(body, name, grant=16, **kwargs):
    params = pltpu.CompilerParams(vmem_limit_bytes=grant * 1024 * 1024)
    return pl.pallas_call(body, name=name, compiler_params=params, **kwargs)


def copies(count):
    return pltpu.SemaphoreType.DMA((count,))


def like(shape, dtype):
    return jax.ShapeDtypeStruct(shape, dtype)


def add_blocks(me, got, own):
    total = own
    for j in range(got.shape[0]):
        total = total + jnp.where(me == j, 0.0, got[j].astype(F32))
    return total


def half_columns(core, rows, i):
    half = rows // NC
    return pl.ds(pl.multiple_of(lax.rem(core + i, NC) * half, half), half)


def encode(core, me, enc, bias, acts_t, loads_of_acts=4, steps=2):
    feat, lat = enc.shape
    rows = acts_t.shape[1]
    half = rows // NC
    part = lat // (NY * NXH)
    piece = feat // loads_of_acts
    size = lat // steps

    def body(c, m, e_hbm, b, a_hbm, out_hbm, own_hbm, acts, e, e_rows, b_rows, out, own, e_sem, a_sems, out_sems):
        loads = [pltpu.make_async_copy(e_hbm, e, e_sem.at[0])]
        for i in range(loads_of_acts):
            here = slice(i * piece, (i + 1) * piece)
            loads.append(pltpu.make_async_copy(a_hbm.at[here], acts.at[here], a_sems.at[i]))
        for load in loads:
            load.start()
        b_rows[...] = jnp.broadcast_to(b[...], (128, lat)).T
        loads[0].wait()
        e_rows[...] = e[...].T
        for load in loads[1:]:
            load.wait()
        stores = []
        for i in range(steps):
            here = slice(i * size, (i + 1) * size)
            for j in range(NC):
                side = slice(j * half, (j + 1) * half)
                out[here, side] = dot(e_rows[here], acts[:, half_columns(c[0], rows, j)], ((1,), (0,))).astype(BF16)
            stores.append(pltpu.make_async_copy(out.at[here], out_hbm.at[here], out_sems.at[i]))
            stores[i].start()
        mine = pl.ds(pl.multiple_of(m[0] * part, part), part)
        for j in range(NC):
            side = slice(j * half, (j + 1) * half)
            own[:, side] = dot(e_rows[mine], acts[:, half_columns(c[0], rows, j)], ((1,), (0,))) + b_rows[mine][:, :1]
        stores.append(pltpu.make_async_copy(own, own_hbm, out_sems.at[steps]))
        stores[steps].start()
        for store in stores:
            store.wait()

    return local_call(
        body, "encode", grant=ALONE,
        out_shape=(like((lat, rows), BF16), like((part, rows), F32)),
        in_specs=[SMEM, SMEM, HBM, VMEM, HBM],
        out_specs=(HBM, HBM),
        scratch_shapes=[
            pltpu.VMEM((feat, rows), BF16),
            pltpu.VMEM((feat, lat), BF16),
            pltpu.VMEM((lat, feat), BF16),
            pltpu.VMEM((lat, 128), F32),
            pltpu.VMEM((lat, rows), BF16),
            pltpu.VMEM((part, rows), F32),
            copies(1),
            copies(loads_of_acts),
            copies(steps + 1),
        ],
    )(core, me, enc, bias, acts_t)


def activate(me, got, own):
    n, part, rows = got.shape

    def body(m, g, o, codes, slope):
        pre = add_blocks(m[0], g, o[...])
        tail = jnp.exp(-jnp.abs(pre))
        value = (jnp.maximum(pre, 0.0) + jnp.log1p(tail)).astype(BF16)
        slope[...] = jnp.where(pre >= 0, 1.0, tail) / (1.0 + tail)
        for j in range(n):
            codes[j] = value

    return local_call(
        body, "activate",
        out_shape=(like((n, part, rows), BF16), like((part, rows), F32)),
        in_specs=[SMEM, VMEM, VMEM],
        out_specs=(VMEM, VMEM),
    )(me, got, own)


def merge_cores(near, own, arrived):
    n, block, half = own.shape

    def body(m, o, a, out, kept):
        for j in range(n):
            out[j] = (o[j] + a[j].astype(F32)).astype(BF16)
        kept[...] = o[m[0]] + a[m[0]].astype(F32)

    return local_call(
        body, "merge_cores",
        out_shape=(like((n, block, half), BF16), like((block, half), F32)),
        in_specs=[SMEM, VMEM, VMEM],
        out_specs=(VMEM, VMEM),
    )(near, own, arrived)


def near_sum(me, got, own, count):
    block, half = own.shape

    def body(m, g, o, out):
        total = add_blocks(m[0], g, o[...]).astype(BF16)
        for j in range(count):
            out[j] = total

    return local_call(
        body, "near_sum",
        out_shape=like((count, block, half), BF16),
        in_specs=[SMEM, VMEM, VMEM],
        out_specs=VMEM,
    )(me, got, own)


def error(got, bias, acts, factor, count):
    n, block, half = got.shape

    def body(f, g, b, a, out):
        recon = g[0].astype(F32)
        for j in range(1, n):
            recon = recon + g[j].astype(F32)
        err = (f[0] * (recon + b[...] - a[...].astype(F32))).astype(BF16)
        for j in range(count):
            out[j] = err

    return local_call(
        body, "error",
        out_shape=like((count, block, half), BF16),
        in_specs=[SMEM, VMEM, VMEM, VMEM],
        out_specs=VMEM,
    )(factor, got, bias, acts)


def squares_and_rows(dec_t):
    feat, lat = dec_t.shape

    def body(d, squares, d_rows):
        wide = d[...].astype(F32)
        squares[...] = jnp.sum(wide * wide, axis=0, keepdims=True)
        d_rows[...] = d[...].T

    return local_call(
        body, "squares_and_rows",
        out_shape=(like((1, lat), F32), like((lat, feat), BF16)),
        in_specs=[VMEM],
        out_specs=(VMEM, VMEM),
    )(dec_t)


def back_half(dec, err, side, filled=None):
    lat, feat = dec.shape
    half = err.shape[1]
    steps = 2
    size = lat // steps

    def body(d, e, *refs):
        out_hbm, out, sems = refs[-3:]
        stores = []
        for i in range(steps):
            here = slice(i * size, (i + 1) * size)
            out[here] = dot(d[here], e[...], ((1,), (0,))).astype(BF16)
            there = out_hbm.at[here, side * half : (side + 1) * half]
            stores.append(pltpu.make_async_copy(out.at[here], there, sems.at[i]))
            stores[i].start()
        for store in stores:
            store.wait()

    more = [] if filled is None else [filled]
    return local_call(
        body, "back_half",
        out_shape=like((lat, NC * half), BF16),
        in_specs=[VMEM, VMEM] + [HBM] * len(more),
        out_specs=HBM,
        scratch_shapes=[pltpu.VMEM((lat, half), BF16), copies(steps)],
        input_output_aliases={2: 0} if more else {},
    )(dec, err, *more)


def at_hand(me, norms, slope, factor):
    part, rows = slope.shape
    lat = norms.shape[1]

    def body(m, f, n, s, penalty, kept, columns):
        columns[...] = jnp.broadcast_to(f[0] * n[...], (128, lat)).T
        penalty[...] = columns[pl.ds(pl.multiple_of(m[0] * part, part), part)][:, :1]
        kept[...] = s[...]

    return local_call(
        body, "at_hand",
        out_shape=(like((part, 1), F32), like((part, rows), F32)),
        in_specs=[SMEM, SMEM, VMEM, VMEM],
        out_specs=(VMEM, VMEM),
        scratch_shapes=[pltpu.VMEM((lat, 128), F32)],
    )(me, factor, norms, slope)


def weigh(got, penalty, slope):
    n, part, rows = got.shape

    def body(g, p, s, out):
        back = g[0].astype(F32)
        for j in range(1, n):
            back = back + g[j].astype(F32)
        value = ((back + p[...]) * s[...]).astype(BF16)
        for j in range(n):
            out[j] = value

    return local_call(
        body, "weigh",
        out_shape=like((n, part, rows), BF16),
        in_specs=[VMEM, VMEM, VMEM],
        out_specs=VMEM,
    )(got, penalty, slope)


def encoder_grads(core, acts_t, delta, steps=3):
    feat, rows = acts_t.shape
    lat = delta.shape[0]
    size = feat // steps
    half = rows // NC

    def body(c, a, d, weight_hbm, bias, weight, sems):
        stores = []
        for i in range(steps):
            here = slice(i * size, (i + 1) * size)
            first, second = (
                dot(a[here, half_columns(c[0], rows, j)], d[:, j * half : (j + 1) * half], ((1,), (1,)))
                for j in range(NC)
            )
            weight[here] = first + second
            stores.append(pltpu.make_async_copy(weight.at[here], weight_hbm.at[here], sems.at[i]))
            stores[i].start()
        bias[...] = dot(jnp.ones((8, rows), BF16), d[...], ((1,), (1,)))[:1]
        for store in stores:
            store.wait()

    return local_call(
        body, "encoder_grads",
        out_shape=(like((feat, lat), F32), like((1, lat), F32)),
        in_specs=[SMEM, VMEM, VMEM],
        out_specs=(HBM, VMEM),
        scratch_shapes=[pltpu.VMEM((feat, lat), F32), copies(steps)],
    )(core, acts_t, delta)


def exchange(x, axis, groups=None):
    return lax.all_to_all(x, axis, 0, 0, axis_index_groups=groups, tiled=True)


def per_device(acts, enc_weight, enc_bias, dec_weight, dec_bias):
    rows, feat = acts.shape
    lat = enc_weight.shape[1]
    scale = 1.0 / jnp.sqrt(F32(rows))
    sparsity = 1.0
    me_layer = lax.axis_index("layer")
    me_latent = lax.axis_index("latent")
    n_layer = NY * NXH
    n_near = ZLO * NXL
    part = lat // n_layer
    core = lax.rem(me_latent, NC)
    x_lo = lax.rem(lax.div(me_latent, NC), NXL)
    z = lax.div(me_latent, NC * NXL)
    near = lax.rem(z + 2 * core, ZLO) * NXL + x_lo
    half = rows // NC
    block = feat // n_near
    core_ref = core[None].astype(jnp.int32)
    layer_ref = me_layer[None].astype(jnp.int32)
    near_ref = near[None].astype(jnp.int32)

    acts_t = acts.T
    dec_t = dec_weight.T
    with jax.named_scope("encode"):
        partial_pre, own_pre = encode(core_ref, layer_ref, enc_weight, enc_bias.reshape(1, lat), acts_t)
        got = exchange(partial_pre.reshape(n_layer, part, rows), "layer")
        codes_part, slope = activate(layer_ref, got, own_pre)
        codes = exchange(codes_part, "layer").reshape(lat, rows)

    with jax.named_scope("decode"):
        away = dot(dec_t, codes[:, half:], ((1,), (0,))).astype(BF16)
        arrived = lax.ppermute(away, "latent", CORE)
        recon = dot(dec_t, codes[:, :half], ((1,), (0,)))
        shape = (n_near, block, half)
        recon, own_recon = merge_cores(near_ref, recon.reshape(shape), arrived.reshape(shape))
        got = exchange(recon, "latent", NEAR)
        recon = near_sum(near_ref, got, own_recon, ZHI)

    with jax.named_scope("norms"):
        late_dec_t, recon = lax.optimization_barrier((dec_t, recon))
        squares, dec_rows = squares_and_rows(late_dec_t)
        squares = squares.reshape(lat)
        for pairs in LAYER_STEPS:
            squares = squares + lax.ppermute(squares, "layer", pairs)
        norms = jnp.sqrt(squares + 1e-06)

    with jax.named_scope("error"):
        got = exchange(recon, "latent", FAR)
        own_dec_bias = lax.dynamic_slice_in_dim(dec_bias, near * block, block, 0)
        acts_part = lax.dynamic_slice(acts_t, (near * block, core * half), (block, half))
        err = error(got, own_dec_bias[:, None], acts_part, (2.0 * scale)[None], n_near)
        err, norms = lax.optimization_barrier((err, norms))
        err_own = exchange(err, "latent", NEAR).reshape(feat, half)
        err_other = lax.ppermute(err_own, "latent", CORE)

    with jax.named_scope("back"):
        partial_back = back_half(dec_rows, err_own, 0)
        partial_back = back_half(dec_rows, err_other, 1, partial_back)
        got = exchange(partial_back.reshape(n_layer, part, rows), "layer")

    with jax.named_scope("decoder_grads"):
        grad_dec_bias = jnp.sum(err_own.astype(F32), axis=1) + jnp.sum(err_other.astype(F32), axis=1)
        column = jnp.sum(codes.astype(F32), axis=1)
        err_t = jnp.concatenate([err_own, err_other], axis=1)
        grad_dec = dot(err_t, codes, ((1,), (1,)))
        grad_dec = grad_dec + (sparsity * scale * column / norms)[None, :] * dec_t.astype(F32)

    with jax.named_scope("encoder_grads"):
        late_slope, grad_dec, grad_dec_bias = lax.optimization_barrier((slope, grad_dec, grad_dec_bias))
        factor = (sparsity * scale)[None]
        penalty, late_slope = at_hand(layer_ref, norms.reshape(1, lat), late_slope, factor)
        got, penalty, late_slope = lax.optimization_barrier((got, penalty, late_slope))
        delta_part = weigh(got, penalty, late_slope)
        delta = exchange(delta_part, "layer").reshape(lat, rows)
        grad_enc, grad_enc_bias = encoder_grads(core_ref, acts_t, delta)
    return (grad_enc, grad_enc_bias.reshape(lat), grad_dec.T, grad_dec_bias)


def solution(mesh):
    return jax.shard_map(
        per_device,
        mesh=mesh,
        in_specs=(
            P(None, "layer"),
            P("layer", "latent"),
            P("latent"),
            P("latent", "layer"),
            P("layer"),
        ),
        out_specs=(P("layer", "latent"), P("latent"), P("latent", "layer"), P("layer")),
        check_vma=False,
    )
```

```python
import jax
import jax.numpy as jnp
from jax import lax
from jax.experimental import pallas as pl
from jax.experimental.pallas import tpu as pltpu
from jax.sharding import PartitionSpec as P

NZ, NXL, NC = 16, 2, 2
NY, NXH = 4, 2
ZLO = 4
ZHI = NZ // ZLO


def latent_index(z, xl, c):
    return (z * NXL + xl) * NC + c


def layer_index(y, xh):
    return y * NXH + xh


NEAR = [
    [latent_index((zh * ZLO + zl - 2 * c) % NZ, xl, c) for zl in range(ZLO) for xl in range(NXL)]
    for zh in range(ZHI)
    for c in range(NC)
]
FAR = [
    [latent_index(zh * ZLO + zl, xl, c) for zh in range(ZHI)]
    for zl in range(ZLO)
    for xl in range(NXL)
    for c in range(NC)
]
CORE = [
    (latent_index(z, xl, c), latent_index(z, xl, 1 - c))
    for z in range(NZ)
    for xl in range(NXL)
    for c in range(NC)
]
LAYER_STEPS = [
    [(layer_index(y, xh), layer_index(y ^ 1, xh)) for y in range(NY) for xh in range(NXH)],
    [(layer_index(y, xh), layer_index(3 - y, xh)) for y in range(NY) for xh in range(NXH)],
    [(layer_index(y, xh), layer_index(y, 1 - xh)) for y in range(NY) for xh in range(NXH)],
]

F32 = jnp.float32
BF16 = jnp.bfloat16


def dot(a, b, dims):
    return lax.dot_general(a, b, (dims, ((), ())), preferred_element_type=F32)


VMEM = pl.BlockSpec(memory_space=pltpu.VMEM)
SMEM = pl.BlockSpec(memory_space=pltpu.SMEM)
HBM = pl.BlockSpec(memory_space=pltpu.HBM)
ALONE = 58


def local_call(body, name, grant=16, **kwargs):
    params = pltpu.CompilerParams(vmem_limit_bytes=grant * 1024 * 1024)
    return pl.pallas_call(body, name=name, compiler_params=params, **kwargs)


def copies(count):
    return pltpu.SemaphoreType.DMA((count,))


def like(shape, dtype):
    return jax.ShapeDtypeStruct(shape, dtype)


def add_blocks(me, got, own):
    total = own
    for j in range(got.shape[0]):
        total = total + jnp.where(me == j, 0.0, got[j].astype(F32))
    return total


def half_columns(core, rows, i):
    half = rows // NC
    return pl.ds(pl.multiple_of(lax.rem(core + i, NC) * half, half), half)


def encode(core, me, enc, bias, acts_t, loads_of_acts=4, steps=2):
    feat, lat = enc.shape
    rows = acts_t.shape[1]
    half = rows // NC
    part = lat // (NY * NXH)
    piece = feat // loads_of_acts
    size = lat // steps

    def body(c, m, e_hbm, b_hbm, a_hbm, out_hbm, own_hbm, acts, e, e_rows, b, b_rows, out, own, e_sem, a_sems, out_sems):
        loads = [pltpu.make_async_copy(e_hbm, e, e_sem.at[0])]
        for i in range(loads_of_acts):
            here = slice(i * piece, (i + 1) * piece)
            loads.append(pltpu.make_async_copy(a_hbm.at[here], acts.at[here], a_sems.at[i]))
        loads.append(pltpu.make_async_copy(b_hbm, b, e_sem.at[1]))
        for load in loads:
            load.start()
        loads[0].wait()
        e_rows[...] = e[...].T
        for load in loads[1:]:
            load.wait()
        stores = []
        for i in range(steps):
            here = slice(i * size, (i + 1) * size)
            for j in range(NC):
                side = slice(j * half, (j + 1) * half)
                out[here, side] = dot(e_rows[here], acts[:, half_columns(c[0], rows, j)], ((1,), (0,))).astype(BF16)
            stores.append(pltpu.make_async_copy(out.at[here], out_hbm.at[here], out_sems.at[i]))
            stores[i].start()
        b_rows[...] = jnp.broadcast_to(b[...], (128, lat)).T
        mine = pl.ds(pl.multiple_of(m[0] * part, part), part)
        for j in range(NC):
            side = slice(j * half, (j + 1) * half)
            own[:, side] = dot(e_rows[mine], acts[:, half_columns(c[0], rows, j)], ((1,), (0,))) + b_rows[mine][:, :1]
        stores.append(pltpu.make_async_copy(own, own_hbm, out_sems.at[steps]))
        stores[steps].start()
        for store in stores:
            store.wait()

    return local_call(
        body, "encode", grant=ALONE,
        out_shape=(like((lat, rows), BF16), like((part, rows), F32)),
        in_specs=[SMEM, SMEM, HBM, HBM, HBM],
        out_specs=(HBM, HBM),
        scratch_shapes=[
            pltpu.VMEM((feat, rows), BF16),
            pltpu.VMEM((feat, lat), BF16),
            pltpu.VMEM((lat, feat), BF16),
            pltpu.VMEM((1, lat), F32),
            pltpu.VMEM((lat, 128), F32),
            pltpu.VMEM((lat, rows), BF16),
            pltpu.VMEM((part, rows), F32),
            copies(2),
            copies(loads_of_acts),
            copies(steps + 1),
        ],
    )(core, me, enc, bias, acts_t)


def activate(me, got, own):
    n, part, rows = got.shape

    def body(m, g, o, codes, slope):
        pre = add_blocks(m[0], g, o[...])
        tail = jnp.exp(-jnp.abs(pre))
        value = (jnp.maximum(pre, 0.0) + jnp.log1p(tail)).astype(BF16)
        slope[...] = jnp.where(pre >= 0, 1.0, tail) / (1.0 + tail)
        for j in range(n):
            codes[j] = value

    return local_call(
        body, "activate",
        out_shape=(like((n, part, rows), BF16), like((part, rows), F32)),
        in_specs=[SMEM, VMEM, VMEM],
        out_specs=(VMEM, VMEM),
    )(me, got, own)


def merge_cores(near, own, arrived):
    n, block, half = own.shape

    def body(m, o, a, out, kept):
        for j in range(n):
            out[j] = (o[j] + a[j].astype(F32)).astype(BF16)
        kept[...] = o[m[0]] + a[m[0]].astype(F32)

    return local_call(
        body, "merge_cores",
        out_shape=(like((n, block, half), BF16), like((block, half), F32)),
        in_specs=[SMEM, VMEM, VMEM],
        out_specs=(VMEM, VMEM),
    )(near, own, arrived)


def near_sum(me, got, own, count):
    block, half = own.shape

    def body(m, g, o, out):
        total = add_blocks(m[0], g, o[...]).astype(BF16)
        for j in range(count):
            out[j] = total

    return local_call(
        body, "near_sum",
        out_shape=like((count, block, half), BF16),
        in_specs=[SMEM, VMEM, VMEM],
        out_specs=VMEM,
    )(me, got, own)


def error(got, bias, acts, factor, count):
    n, block, half = got.shape

    def body(f, g, b, a, out):
        recon = g[0].astype(F32)
        for j in range(1, n):
            recon = recon + g[j].astype(F32)
        err = (f[0] * (recon + b[...] - a[...].astype(F32))).astype(BF16)
        for j in range(count):
            out[j] = err

    return local_call(
        body, "error",
        out_shape=like((count, block, half), BF16),
        in_specs=[SMEM, VMEM, VMEM, VMEM],
        out_specs=VMEM,
    )(factor, got, bias, acts)


def squares_and_rows(dec_t):
    feat, lat = dec_t.shape

    def body(d, squares, d_rows):
        wide = d[...].astype(F32)
        squares[...] = jnp.sum(wide * wide, axis=0, keepdims=True)
        d_rows[...] = d[...].T

    return local_call(
        body, "squares_and_rows",
        out_shape=(like((1, lat), F32), like((lat, feat), BF16)),
        in_specs=[VMEM],
        out_specs=(VMEM, VMEM),
    )(dec_t)


def back_half(dec, err, side, filled=None):
    lat, feat = dec.shape
    half = err.shape[1]
    steps = 2
    size = lat // steps

    def body(d, e, *refs):
        out_hbm, out, sems = refs[-3:]
        stores = []
        for i in range(steps):
            here = slice(i * size, (i + 1) * size)
            out[here] = dot(d[here], e[...], ((1,), (0,))).astype(BF16)
            there = out_hbm.at[here, side * half : (side + 1) * half]
            stores.append(pltpu.make_async_copy(out.at[here], there, sems.at[i]))
            stores[i].start()
        for store in stores:
            store.wait()

    more = [] if filled is None else [filled]
    return local_call(
        body, "back_half",
        out_shape=like((lat, NC * half), BF16),
        in_specs=[VMEM, VMEM] + [HBM] * len(more),
        out_specs=HBM,
        scratch_shapes=[pltpu.VMEM((lat, half), BF16), copies(steps)],
        input_output_aliases={2: 0} if more else {},
    )(dec, err, *more)


def at_hand(me, norms, slope, factor):
    part, rows = slope.shape
    lat = norms.shape[1]

    def body(m, f, n, s, penalty, kept, columns):
        columns[...] = jnp.broadcast_to(f[0] * n[...], (128, lat)).T
        penalty[...] = columns[pl.ds(pl.multiple_of(m[0] * part, part), part)][:, :1]
        kept[...] = s[...]

    return local_call(
        body, "at_hand",
        out_shape=(like((part, 1), F32), like((part, rows), F32)),
        in_specs=[SMEM, SMEM, VMEM, VMEM],
        out_specs=(VMEM, VMEM),
        scratch_shapes=[pltpu.VMEM((lat, 128), F32)],
    )(me, factor, norms, slope)


def weigh(got, penalty, slope):
    n, part, rows = got.shape

    def body(g, p, s, out):
        back = g[0].astype(F32)
        for j in range(1, n):
            back = back + g[j].astype(F32)
        value = ((back + p[...]) * s[...]).astype(BF16)
        for j in range(n):
            out[j] = value

    return local_call(
        body, "weigh",
        out_shape=like((n, part, rows), BF16),
        in_specs=[VMEM, VMEM, VMEM],
        out_specs=VMEM,
    )(got, penalty, slope)


def encoder_grads(core, acts_t, delta, steps=2):
    feat, rows = acts_t.shape
    lat = delta.shape[0]
    size = feat // steps
    half = rows // NC

    def body(c, a, d, weight_hbm, bias, weight, sems):
        stores = []
        for i in range(steps):
            here = slice(i * size, (i + 1) * size)
            first, second = (
                dot(a[here, half_columns(c[0], rows, j)], d[:, j * half : (j + 1) * half], ((1,), (1,)))
                for j in range(NC)
            )
            weight[here] = first + second
            stores.append(pltpu.make_async_copy(weight.at[here], weight_hbm.at[here], sems.at[i]))
            stores[i].start()
        bias[...] = dot(jnp.ones((8, rows), BF16), d[...], ((1,), (1,)))[:1]
        for store in stores:
            store.wait()

    return local_call(
        body, "encoder_grads",
        out_shape=(like((feat, lat), F32), like((1, lat), F32)),
        in_specs=[SMEM, VMEM, VMEM],
        out_specs=(HBM, VMEM),
        scratch_shapes=[pltpu.VMEM((feat, lat), F32), copies(steps)],
    )(core, acts_t, delta)


def exchange(x, axis, groups=None):
    return lax.all_to_all(x, axis, 0, 0, axis_index_groups=groups, tiled=True)


def per_device(acts, enc_weight, enc_bias, dec_weight, dec_bias):
    rows, feat = acts.shape
    lat = enc_weight.shape[1]
    scale = 1.0 / jnp.sqrt(F32(rows))
    sparsity = 1.0
    me_layer = lax.axis_index("layer")
    me_latent = lax.axis_index("latent")
    n_layer = NY * NXH
    n_near = ZLO * NXL
    part = lat // n_layer
    core = lax.rem(me_latent, NC)
    x_lo = lax.rem(lax.div(me_latent, NC), NXL)
    z = lax.div(me_latent, NC * NXL)
    near = lax.rem(z + 2 * core, ZLO) * NXL + x_lo
    half = rows // NC
    block = feat // n_near
    core_ref = core[None].astype(jnp.int32)
    layer_ref = me_layer[None].astype(jnp.int32)
    near_ref = near[None].astype(jnp.int32)

    acts_t = acts.T
    dec_t = dec_weight.T
    with jax.named_scope("encode"):
        partial_pre, own_pre = encode(core_ref, layer_ref, enc_weight, enc_bias.reshape(1, lat), acts_t)
        got = exchange(partial_pre.reshape(n_layer, part, rows), "layer")
        codes_part, slope = activate(layer_ref, got, own_pre)
        codes = exchange(codes_part, "layer").reshape(lat, rows)

    with jax.named_scope("decode"):
        away = dot(dec_t, codes[:, half:], ((1,), (0,))).astype(BF16)
        arrived = lax.ppermute(away, "latent", CORE)
        recon = dot(dec_t, codes[:, :half], ((1,), (0,)))
        shape = (n_near, block, half)
        recon, own_recon = merge_cores(near_ref, recon.reshape(shape), arrived.reshape(shape))
        got = exchange(recon, "latent", NEAR)
        recon = near_sum(near_ref, got, own_recon, ZHI)

    with jax.named_scope("norms"):
        late_dec_t, recon = lax.optimization_barrier((dec_t, recon))
        squares, dec_rows = squares_and_rows(late_dec_t)
        squares = squares.reshape(lat)
        for pairs in LAYER_STEPS:
            squares = squares + lax.ppermute(squares, "layer", pairs)
        norms = jnp.sqrt(squares + 1e-06)

    with jax.named_scope("error"):
        got = exchange(recon, "latent", FAR)
        own_dec_bias = lax.dynamic_slice_in_dim(dec_bias, near * block, block, 0)
        acts_part = lax.dynamic_slice(acts_t, (near * block, core * half), (block, half))
        err = error(got, own_dec_bias[:, None], acts_part, (2.0 * scale)[None], n_near)
        err, norms = lax.optimization_barrier((err, norms))
        err_own = exchange(err, "latent", NEAR).reshape(feat, half)
        err_other = lax.ppermute(err_own, "latent", CORE)

    with jax.named_scope("back"):
        partial_back = back_half(dec_rows, err_own, 0)
        partial_back = back_half(dec_rows, err_other, 1, partial_back)
        got = exchange(partial_back.reshape(n_layer, part, rows), "layer")

    with jax.named_scope("decoder_grads"):
        grad_dec_bias = jnp.sum(err_own.astype(F32), axis=1) + jnp.sum(err_other.astype(F32), axis=1)
        column = jnp.sum(codes.astype(F32), axis=1)
        err_t = jnp.concatenate([err_own, err_other], axis=1)
        grad_dec = dot(err_t, codes, ((1,), (1,)))
        grad_dec = grad_dec + (sparsity * scale * column / norms)[None, :] * dec_t.astype(F32)

    with jax.named_scope("encoder_grads"):
        late_slope, grad_dec, grad_dec_bias = lax.optimization_barrier((slope, grad_dec, grad_dec_bias))
        factor = (sparsity * scale)[None]
        penalty, late_slope = at_hand(layer_ref, norms.reshape(1, lat), late_slope, factor)
        got, penalty, late_slope = lax.optimization_barrier((got, penalty, late_slope))
        delta_part = weigh(got, penalty, late_slope)
        delta = exchange(delta_part, "layer").reshape(lat, rows)
        grad_enc, grad_enc_bias = encoder_grads(core_ref, acts_t, delta)
    return (grad_enc, grad_enc_bias.reshape(lat), grad_dec.T, grad_dec_bias)


def solution(mesh):
    return jax.shard_map(
        per_device,
        mesh=mesh,
        in_specs=(
            P(None, "layer"),
            P("layer", "latent"),
            P("latent"),
            P("latent", "layer"),
            P("layer"),
        ),
        out_specs=(P("layer", "latent"), P("latent"), P("latent", "layer"), P("layer")),
        check_vma=False,
    )
```

```python
import jax
import jax.numpy as jnp
from jax import lax
from jax.experimental import pallas as pl
from jax.experimental.pallas import tpu as pltpu
from jax.sharding import PartitionSpec as P

NZ, NXL, NC = 16, 2, 2
NY, NXH = 4, 2
ZLO = 4
ZHI = NZ // ZLO


def latent_index(z, xl, c):
    return (z * NXL + xl) * NC + c


def layer_index(y, xh):
    return y * NXH + xh


NEAR = [
    [latent_index((zh * ZLO + zl - 2 * c) % NZ, xl, c) for zl in range(ZLO) for xl in range(NXL)]
    for zh in range(ZHI)
    for c in range(NC)
]
FAR = [
    [latent_index(zh * ZLO + zl, xl, c) for zh in range(ZHI)]
    for zl in range(ZLO)
    for xl in range(NXL)
    for c in range(NC)
]
CORE = [
    (latent_index(z, xl, c), latent_index(z, xl, 1 - c))
    for z in range(NZ)
    for xl in range(NXL)
    for c in range(NC)
]
LAYER_STEPS = [
    [(layer_index(y, xh), layer_index(y ^ 1, xh)) for y in range(NY) for xh in range(NXH)],
    [(layer_index(y, xh), layer_index(3 - y, xh)) for y in range(NY) for xh in range(NXH)],
    [(layer_index(y, xh), layer_index(y, 1 - xh)) for y in range(NY) for xh in range(NXH)],
]

F32 = jnp.float32
BF16 = jnp.bfloat16


def dot(a, b, dims):
    return lax.dot_general(a, b, (dims, ((), ())), preferred_element_type=F32)


VMEM = pl.BlockSpec(memory_space=pltpu.VMEM)
SMEM = pl.BlockSpec(memory_space=pltpu.SMEM)
HBM = pl.BlockSpec(memory_space=pltpu.HBM)
ALONE = 58


def local_call(body, name, grant=16, **kwargs):
    params = pltpu.CompilerParams(vmem_limit_bytes=grant * 1024 * 1024)
    return pl.pallas_call(body, name=name, compiler_params=params, **kwargs)


def copies(count):
    return pltpu.SemaphoreType.DMA((count,))


def like(shape, dtype):
    return jax.ShapeDtypeStruct(shape, dtype)


def add_blocks(me, got, own):
    total = own
    for j in range(got.shape[0]):
        total = total + jnp.where(me == j, 0.0, got[j].astype(F32))
    return total


def half_columns(core, rows, i):
    half = rows // NC
    return pl.ds(pl.multiple_of(lax.rem(core + i, NC) * half, half), half)


def encode(core, enc, acts_t, loads_of_acts=4, steps=2):
    feat, lat = enc.shape
    rows = acts_t.shape[1]
    half = rows // NC
    piece = feat // loads_of_acts
    size = lat // steps

    def body(c, e_hbm, a_hbm, out_hbm, acts, e, e_rows, out, e_sem, a_sems, out_sems):
        loads = [pltpu.make_async_copy(e_hbm, e, e_sem.at[0])]
        for i in range(loads_of_acts):
            here = slice(i * piece, (i + 1) * piece)
            loads.append(pltpu.make_async_copy(a_hbm.at[here], acts.at[here], a_sems.at[i]))
        for load in loads:
            load.start()
        loads[0].wait()
        e_rows[...] = e[...].T
        for load in loads[1:]:
            load.wait()
        stores = []
        for i in range(steps):
            here = slice(i * size, (i + 1) * size)
            for j in range(NC):
                side = slice(j * half, (j + 1) * half)
                out[here, side] = dot(e_rows[here], acts[:, half_columns(c[0], rows, j)], ((1,), (0,))).astype(BF16)
            stores.append(pltpu.make_async_copy(out.at[here], out_hbm.at[here], out_sems.at[i]))
            stores[i].start()
        for store in stores:
            store.wait()

    return local_call(
        body, "encode", grant=ALONE,
        out_shape=like((lat, rows), BF16),
        in_specs=[SMEM, HBM, HBM],
        out_specs=HBM,
        scratch_shapes=[
            pltpu.VMEM((feat, rows), BF16),
            pltpu.VMEM((feat, lat), BF16),
            pltpu.VMEM((lat, feat), BF16),
            pltpu.VMEM((lat, rows), BF16),
            copies(1),
            copies(loads_of_acts),
            copies(steps),
        ],
    )(core, enc, acts_t)


def own_block(core, me, enc, bias, acts_t):
    feat, lat = enc.shape
    rows = acts_t.shape[1]
    half = rows // NC
    part = lat // (NY * NXH)

    def body(c, m, e_hbm, b_hbm, a_hbm, own, acts, e, e_rows, b, b_rows, sems):
        loads = [
            pltpu.make_async_copy(e_hbm, e, sems.at[0]),
            pltpu.make_async_copy(b_hbm, b, sems.at[1]),
            pltpu.make_async_copy(a_hbm, acts, sems.at[2]),
        ]
        for load in loads:
            load.start()
        for load in loads:
            load.wait()
        e_rows[...] = e[...].T
        b_rows[...] = jnp.broadcast_to(b[...], (128, lat)).T
        mine = pl.ds(pl.multiple_of(m[0] * part, part), part)
        for j in range(NC):
            side = slice(j * half, (j + 1) * half)
            own[:, side] = dot(e_rows[mine], acts[:, half_columns(c[0], rows, j)], ((1,), (0,))) + b_rows[mine][:, :1]

    return local_call(
        body, "own_block", grant=ALONE,
        out_shape=like((part, rows), F32),
        in_specs=[SMEM, SMEM, HBM, HBM, HBM],
        out_specs=VMEM,
        scratch_shapes=[
            pltpu.VMEM((feat, rows), BF16),
            pltpu.VMEM((feat, lat), BF16),
            pltpu.VMEM((lat, feat), BF16),
            pltpu.VMEM((1, lat), F32),
            pltpu.VMEM((lat, 128), F32),
            copies(3),
        ],
    )(core, me, enc, bias, acts_t)


def activate(me, got, own):
    n, part, rows = got.shape

    def body(m, g, o, codes, slope):
        pre = add_blocks(m[0], g, o[...])
        tail = jnp.exp(-jnp.abs(pre))
        value = (jnp.maximum(pre, 0.0) + jnp.log1p(tail)).astype(BF16)
        slope[...] = jnp.where(pre >= 0, 1.0, tail) / (1.0 + tail)
        for j in range(n):
            codes[j] = value

    return local_call(
        body, "activate",
        out_shape=(like((n, part, rows), BF16), like((part, rows), F32)),
        in_specs=[SMEM, VMEM, VMEM],
        out_specs=(VMEM, VMEM),
    )(me, got, own)


def merge_cores(near, own, arrived):
    n, block, half = own.shape

    def body(m, o, a, out, kept):
        for j in range(n):
            out[j] = (o[j] + a[j].astype(F32)).astype(BF16)
        kept[...] = o[m[0]] + a[m[0]].astype(F32)

    return local_call(
        body, "merge_cores",
        out_shape=(like((n, block, half), BF16), like((block, half), F32)),
        in_specs=[SMEM, VMEM, VMEM],
        out_specs=(VMEM, VMEM),
    )(near, own, arrived)


def near_sum(me, got, own, count):
    block, half = own.shape

    def body(m, g, o, out):
        total = add_blocks(m[0], g, o[...]).astype(BF16)
        for j in range(count):
            out[j] = total

    return local_call(
        body, "near_sum",
        out_shape=like((count, block, half), BF16),
        in_specs=[SMEM, VMEM, VMEM],
        out_specs=VMEM,
    )(me, got, own)


def error(got, bias, acts, factor, count):
    n, block, half = got.shape

    def body(f, g, b, a, out):
        recon = g[0].astype(F32)
        for j in range(1, n):
            recon = recon + g[j].astype(F32)
        err = (f[0] * (recon + b[...] - a[...].astype(F32))).astype(BF16)
        for j in range(count):
            out[j] = err

    return local_call(
        body, "error",
        out_shape=like((count, block, half), BF16),
        in_specs=[SMEM, VMEM, VMEM, VMEM],
        out_specs=VMEM,
    )(factor, got, bias, acts)


def squares_and_rows(dec_t):
    feat, lat = dec_t.shape

    def body(d, squares, d_rows):
        wide = d[...].astype(F32)
        squares[...] = jnp.sum(wide * wide, axis=0, keepdims=True)
        d_rows[...] = d[...].T

    return local_call(
        body, "squares_and_rows",
        out_shape=(like((1, lat), F32), like((lat, feat), BF16)),
        in_specs=[VMEM],
        out_specs=(VMEM, VMEM),
    )(dec_t)


def back_half(dec, err, side, filled=None):
    lat, feat = dec.shape
    half = err.shape[1]
    steps = 2
    size = lat // steps

    def body(d, e, *refs):
        out_hbm, out, sems = refs[-3:]
        stores = []
        for i in range(steps):
            here = slice(i * size, (i + 1) * size)
            out[here] = dot(d[here], e[...], ((1,), (0,))).astype(BF16)
            there = out_hbm.at[here, side * half : (side + 1) * half]
            stores.append(pltpu.make_async_copy(out.at[here], there, sems.at[i]))
            stores[i].start()
        for store in stores:
            store.wait()

    more = [] if filled is None else [filled]
    return local_call(
        body, "back_half",
        out_shape=like((lat, NC * half), BF16),
        in_specs=[VMEM, VMEM] + [HBM] * len(more),
        out_specs=HBM,
        scratch_shapes=[pltpu.VMEM((lat, half), BF16), copies(steps)],
        input_output_aliases={2: 0} if more else {},
    )(dec, err, *more)


def at_hand(me, norms, slope, factor):
    part, rows = slope.shape
    lat = norms.shape[1]

    def body(m, f, n, s, penalty, kept, columns):
        columns[...] = jnp.broadcast_to(f[0] * n[...], (128, lat)).T
        penalty[...] = columns[pl.ds(pl.multiple_of(m[0] * part, part), part)][:, :1]
        kept[...] = s[...]

    return local_call(
        body, "at_hand",
        out_shape=(like((part, 1), F32), like((part, rows), F32)),
        in_specs=[SMEM, SMEM, VMEM, VMEM],
        out_specs=(VMEM, VMEM),
        scratch_shapes=[pltpu.VMEM((lat, 128), F32)],
    )(me, factor, norms, slope)


def weigh(got, penalty, slope):
    n, part, rows = got.shape

    def body(g, p, s, out):
        back = g[0].astype(F32)
        for j in range(1, n):
            back = back + g[j].astype(F32)
        value = ((back + p[...]) * s[...]).astype(BF16)
        for j in range(n):
            out[j] = value

    return local_call(
        body, "weigh",
        out_shape=like((n, part, rows), BF16),
        in_specs=[VMEM, VMEM, VMEM],
        out_specs=VMEM,
    )(got, penalty, slope)


def encoder_grads(core, acts_t, delta, steps=2):
    feat, rows = acts_t.shape
    lat = delta.shape[0]
    size = feat // steps
    half = rows // NC

    def body(c, a, d, weight_hbm, bias, weight, sems):
        stores = []
        for i in range(steps):
            here = slice(i * size, (i + 1) * size)
            first, second = (
                dot(a[here, half_columns(c[0], rows, j)], d[:, j * half : (j + 1) * half], ((1,), (1,)))
                for j in range(NC)
            )
            weight[here] = first + second
            stores.append(pltpu.make_async_copy(weight.at[here], weight_hbm.at[here], sems.at[i]))
            stores[i].start()
        bias[...] = dot(jnp.ones((8, rows), BF16), d[...], ((1,), (1,)))[:1]
        for store in stores:
            store.wait()

    return local_call(
        body, "encoder_grads",
        out_shape=(like((feat, lat), F32), like((1, lat), F32)),
        in_specs=[SMEM, VMEM, VMEM],
        out_specs=(HBM, VMEM),
        scratch_shapes=[pltpu.VMEM((feat, lat), F32), copies(steps)],
    )(core, acts_t, delta)


def exchange(x, axis, groups=None):
    return lax.all_to_all(x, axis, 0, 0, axis_index_groups=groups, tiled=True)


def per_device(acts, enc_weight, enc_bias, dec_weight, dec_bias):
    rows, feat = acts.shape
    lat = enc_weight.shape[1]
    scale = 1.0 / jnp.sqrt(F32(rows))
    sparsity = 1.0
    me_layer = lax.axis_index("layer")
    me_latent = lax.axis_index("latent")
    n_layer = NY * NXH
    n_near = ZLO * NXL
    part = lat // n_layer
    core = lax.rem(me_latent, NC)
    x_lo = lax.rem(lax.div(me_latent, NC), NXL)
    z = lax.div(me_latent, NC * NXL)
    near = lax.rem(z + 2 * core, ZLO) * NXL + x_lo
    half = rows // NC
    block = feat // n_near
    core_ref = core[None].astype(jnp.int32)
    layer_ref = me_layer[None].astype(jnp.int32)
    near_ref = near[None].astype(jnp.int32)

    acts_t = acts.T
    dec_t = dec_weight.T
    with jax.named_scope("encode"):
        partial_pre = encode(core_ref, enc_weight, acts_t)
        late_bias, partial_pre = lax.optimization_barrier((enc_bias.reshape(1, lat), partial_pre))
        own_pre = own_block(core_ref, layer_ref, enc_weight, late_bias, acts_t)
        got = exchange(partial_pre.reshape(n_layer, part, rows), "layer")
        codes_part, slope = activate(layer_ref, got, own_pre)
        codes = exchange(codes_part, "layer").reshape(lat, rows)

    with jax.named_scope("decode"):
        away = dot(dec_t, codes[:, half:], ((1,), (0,))).astype(BF16)
        arrived = lax.ppermute(away, "latent", CORE)
        recon = dot(dec_t, codes[:, :half], ((1,), (0,)))
        shape = (n_near, block, half)
        recon, own_recon = merge_cores(near_ref, recon.reshape(shape), arrived.reshape(shape))
        got = exchange(recon, "latent", NEAR)
        recon = near_sum(near_ref, got, own_recon, ZHI)

    with jax.named_scope("norms"):
        late_dec_t, recon = lax.optimization_barrier((dec_t, recon))
        squares, dec_rows = squares_and_rows(late_dec_t)
        squares = squares.reshape(lat)
        for pairs in LAYER_STEPS:
            squares = squares + lax.ppermute(squares, "layer", pairs)
        norms = jnp.sqrt(squares + 1e-06)

    with jax.named_scope("error"):
        got = exchange(recon, "latent", FAR)
        own_dec_bias = lax.dynamic_slice_in_dim(dec_bias, near * block, block, 0)
        acts_part = lax.dynamic_slice(acts_t, (near * block, core * half), (block, half))
        err = error(got, own_dec_bias[:, None], acts_part, (2.0 * scale)[None], n_near)
        err, norms = lax.optimization_barrier((err, norms))
        err_own = exchange(err, "latent", NEAR).reshape(feat, half)
        err_other = lax.ppermute(err_own, "latent", CORE)

    with jax.named_scope("back"):
        partial_back = back_half(dec_rows, err_own, 0)
        partial_back = back_half(dec_rows, err_other, 1, partial_back)
        got = exchange(partial_back.reshape(n_layer, part, rows), "layer")

    with jax.named_scope("decoder_grads"):
        grad_dec_bias = jnp.sum(err_own.astype(F32), axis=1) + jnp.sum(err_other.astype(F32), axis=1)
        column = jnp.sum(codes.astype(F32), axis=1)
        err_t = jnp.concatenate([err_own, err_other], axis=1)
        grad_dec = dot(err_t, codes, ((1,), (1,)))
        grad_dec = grad_dec + (sparsity * scale * column / norms)[None, :] * dec_t.astype(F32)

    with jax.named_scope("encoder_grads"):
        late_slope, grad_dec, grad_dec_bias = lax.optimization_barrier((slope, grad_dec, grad_dec_bias))
        factor = (sparsity * scale)[None]
        penalty, late_slope = at_hand(layer_ref, norms.reshape(1, lat), late_slope, factor)
        got, penalty, late_slope = lax.optimization_barrier((got, penalty, late_slope))
        delta_part = weigh(got, penalty, late_slope)
        delta = exchange(delta_part, "layer").reshape(lat, rows)
        grad_enc, grad_enc_bias = encoder_grads(core_ref, acts_t, delta)
    return (grad_enc, grad_enc_bias.reshape(lat), grad_dec.T, grad_dec_bias)


def solution(mesh):
    return jax.shard_map(
        per_device,
        mesh=mesh,
        in_specs=(
            P(None, "layer"),
            P("layer", "latent"),
            P("latent"),
            P("latent", "layer"),
            P("layer"),
        ),
        out_specs=(P("layer", "latent"), P("latent"), P("latent", "layer"), P("layer")),
        check_vma=False,
    )
```
